32 devices in a mesh: seq: 8 (over z, y), tp: 4 (over x, core).
Axes of the slice: x: 2, y: 2, z: 4, core: 2. Of those that a mesh axis runs over, the one named last changes fastest.
Arguments:
- tokens: bfloat16 [2048, 1280], P('seq'), may hold values from -45 to 45
- ln_gain: float32 [1280], replicated, may hold values from 0.6 to 10, as said below
- ln_bias: float32 [1280], replicated, may hold values from -3 to 3
- w_qkv: bfloat16 [3, 1280, 1280], P(None, None, 'tp'), may hold values from -0.15625 to 0.15625
- b_qkv: float32 [3, 1280], P(None, 'tp'), may hold values from -3 to 3
- w_out: bfloat16 [1280, 1280], P('tp'), may hold values from -0.15625 to 0.15625
- b_out: float32 [1280], replicated, may hold values from -3 to 3
- merge_gain: float32 [1280], replicated, may hold values from 0.25 to 1.75
- merge_bias: float32 [1280], replicated, may hold values from -3 to 3
- segments: int32 [512], replicated, may hold values from 0 to 3, never falling along the last dimension, each value on 1 to 256 neighbouring positions
- owners: int32 [512, 1], P('seq'), may hold values from 0 to 7; in each aligned block of 64 rows (0 to 63, 64 to 127, ...) at most 16 rows name the same one
Outputs:
- routed: bfloat16 [1024, 5120], P('seq', 'tp')
The draws below stay inside these ranges and needn't reach their ends.
Inputs may be any that keep to these rules, and one draw needn't show every extreme that they name: `segments`: Non-decreasing along the rows; one image holds at most 256 merged rows, and some image holds exactly that many. `owners`: among the 64 merged rows of one device no owner is named more than 16 times, a bound that some block reaches. `ln_gain`: gains are positive, within 0.6 to 10.
All inputs are finite; a program needn't handle non-finite values.
Results may differ from the reference program's by a relative error of at most 0.024.
The reference program's roundings to bfloat16 on the way count: a program that leaves them out, or rounds other values in their place, can miss the bound.
Values may be sent and summed in bfloat16 or wider, within the bound.
A program may use at most 64 MiB of HBM per device.

```python
import math
import jax
import jax.numpy as jnp
import numpy as np
from jax import lax

D = 1280
HEADS = 16
HEAD_DIM = 80
TOK_DEV = 256
SPAN = 4
TOKENS = 2048
GROUPS = 512
MER_DEV = 64
IMAGES = 4
CAP = 16
N_SEQ = 8
N_TP = 4


def draw_tokens(key, part):
    key_rows, key_cols, key_vals = jax.random.split(key, 3)
    row_scale = jnp.exp(jax.random.uniform(key_rows, (TOKENS, 1), jnp.float32, -1.2, 1.2))
    col_scale = jnp.exp(jax.random.uniform(key_cols, (1, D), jnp.float32, -1.2, 1.2))
    base = jnp.clip(jax.random.normal(key_vals, (TOKENS, D), jnp.float32), -4.0, 4.0)
    return (base * row_scale * col_scale).astype(jnp.bfloat16)


def draw_ln_gain(key, part):
    return jnp.exp(jax.random.uniform(key, (D,), jnp.float32, -0.5, 0.5))


def block_scale(own_key, extent, cuts, least, largest):
    gain, own = 1.0, jax.random.fold_in(own_key, 6)
    for axis_at, parts in cuts:
        draws = jnp.exp(jax.random.uniform(jax.random.fold_in(own, axis_at), (parts,), jnp.float32, least / len(cuts), largest / len(cuts)))
        gain = gain * jnp.repeat(draws, extent[axis_at] // parts).reshape([-1 if axis == axis_at else 1 for axis in range(len(extent))])
    return gain


def length_profile(count, total, reach, skew):
    loads = [(1 << 20) // math.isqrt(rank ** skew) + 1 for rank in range(2, count + 1)]
    surplus, holding = total - reach - (count - 1), [1] * (count - 1)
    while surplus > 0:
        movable = [i for i in range(count - 1) if holding[i] < reach]
        whole, budget = sum([loads[i] for i in movable]), surplus
        for i in movable:
            more = min(reach - holding[i], max(1, budget * loads[i] // whole), surplus)
            holding[i] = holding[i] + more
            surplus = surplus - more
    return np.array([reach] + holding)


def ragged(own_key, number_of, total, limit, lean):
    if number_of == 2:
        one = jax.random.randint(own_key, (), max(1, total - limit), min(limit, total - 1) + 1)
        return jnp.stack([one, total - one])
    sizes = jnp.asarray(length_profile(number_of, total, limit, lean), jnp.int32)
    twos = (number_of - 1) // 2
    donor, taker = sizes[1:1 + 2 * twos:2], sizes[2:2 + 2 * twos:2]
    margin = jnp.minimum(donor - 1, limit - taker)
    passed = jax.random.randint(jax.random.fold_in(own_key, 1), (twos,), 0, 1 << 20) % (margin + 1)
    sizes = sizes.at[1:1 + 2 * twos:2].set(donor - passed).at[2:2 + 2 * twos:2].set(taker + passed)
    return sizes[jax.random.permutation(jax.random.fold_in(own_key, 2), number_of)]


def assign_block(key, own, number, rows, number_of, top, bound, slope):
    order = jax.random.permutation(key, number_of)
    heavy_load, usual = portions_of(number_of, rows * top, bound, slope, True), portions_of(number_of, rows * top, bound, slope, False)
    places = jnp.arange(number_of)

    def named(lengths, turn):
        used = int((lengths > 0).sum())
        fixed = max(1, used // 4)
        passed = fixed + (places - fixed + turn * (used - fixed)) % max(1, number_of - fixed)
        return jnp.zeros((number_of,), jnp.int32).at[order[jnp.where(places < fixed, places, passed)]].set(jnp.asarray(lengths, jnp.int32))

    lengths = jnp.where(number % 4 == 0, named(heavy_load, number // 4), named(usual, number - number // 4 - 1))
    mixed = jax.random.permutation(jax.random.fold_in(own, 3), number_of)
    donor, sink = mixed[0:number_of // 2 * 2:2], mixed[1:number_of // 2 * 2:2]
    margin = jnp.minimum(lengths[donor] - 1, bound - lengths[sink]) // 2
    margin = jnp.where((donor == order[0]) | (sink == order[0]) | (lengths[sink] == 0), 0, jnp.maximum(margin, 0))
    passed = jax.random.randint(jax.random.fold_in(own, 4), (number_of // 2,), 0, 1 << 20) % (margin + 1)
    lengths = lengths.at[donor].add(-passed).at[sink].add(passed)
    members = jnp.searchsorted(jnp.cumsum(lengths), jnp.arange(rows * top), side="right").astype(jnp.int32)
    grid = members.reshape(top, rows).T
    grid = grid[jax.random.permutation(jax.random.fold_in(own, 1), rows)]
    turn = jax.random.randint(jax.random.fold_in(own, 2), (rows, 1), 0, top)
    return jnp.take_along_axis(grid, (jnp.arange(top)[None, :] + turn) % top, axis=1)


def portions_of(amount, total, reach, skew, full):
    loads = [(1 << 20) // math.isqrt(grade ** skew) + 1 for grade in range(1, amount + 1)]
    largest = reach if full else min(reach, max(-(-total // amount), total * loads[0] // sum(loads)))
    least = 1 if total - largest >= amount - 1 else 0
    counts, surplus = [largest] + [least] * (amount - 1), total - largest - least * (amount - 1)
    while surplus > 0:
        free = [i for i in range(1, amount) if counts[i] < largest] or [i for i in range(1, amount) if counts[i] < reach]
        mass, left = sum([loads[i] for i in free]), surplus
        for i in free:
            addition = min(reach - counts[i], max(1, left * loads[i] // mass), surplus)
            counts[i] = counts[i] + addition
            surplus = surplus - addition
    return np.array(counts)


def centred(stream_key, dims, scale, most, cuts=(), kind=jnp.bfloat16):
    factor_of = block_scale(stream_key, dims, cuts, -0.22, 0.18) if cuts else 1.0
    result = jax.random.normal(stream_key, dims, jnp.float32) * scale * factor_of
    return jnp.minimum(jnp.maximum(result, -most), most).astype(kind)


def setup_inputs(seed: int = 0) -> dict:
    key_of = jax.random.split(jax.random.key(seed), 12)
    tokens = draw_tokens(jax.random.fold_in(key_of[11], 71), 0)
    ln_gain = draw_ln_gain(jax.random.fold_in(key_of[11], 71), 0)
    ln_bias = centred(key_of[2], (D,), 0.5, 3.0, (), jnp.float32)
    w_qkv = centred(key_of[3], (3, D, D), D ** -0.5, 0.15625, ((2, 4),))
    b_qkv = centred(key_of[4], (3, D), 0.5, 3.0, ((1, 4),), jnp.float32)
    w_out = centred(key_of[5], (D, D), D ** -0.5, 0.15625, ((0, 4),))
    b_out = centred(key_of[6], (D,), 0.5, 3.0, (), jnp.float32)
    merge_gain = jnp.clip(1.0 + 0.15 * jax.random.normal(key_of[7], (D,), jnp.float32), 0.25, 1.75)
    merge_bias = centred(key_of[8], (D,), 0.5, 3.0, (), jnp.float32)
    segments = jnp.searchsorted(jnp.cumsum(ragged(key_of[9], IMAGES, GROUPS, SPAN * TOK_DEV // 4, 2)), jnp.arange(GROUPS), side="right").astype(jnp.int32)
    owners_keys = jax.random.split(jax.random.fold_in(key_of[10], 1), GROUPS // MER_DEV)
    owners_turns = jax.random.permutation(jax.random.fold_in(key_of[10], 3), GROUPS // MER_DEV)
    owners = jax.vmap(lambda own, number: assign_block(jax.random.fold_in(key_of[10], 2), own, number, MER_DEV, N_SEQ, 1, CAP, 2))(owners_keys, owners_turns).reshape((GROUPS, 1))
    return dict(tokens=tokens, ln_gain=ln_gain, ln_bias=ln_bias, w_qkv=w_qkv, b_qkv=b_qkv, w_out=w_out, b_out=b_out, merge_gain=merge_gain, merge_bias=merge_bias, segments=segments, owners=owners)


epsilon = 1e-06
masked_score = -1e+30

def layer_norm(values, gain_row, shift_row):
    center = lax.optimization_barrier(jnp.mean(values, axis=-1, keepdims=True))
    centered = values - center
    spread = lax.optimization_barrier(jnp.mean(centered * centered, axis=-1, keepdims=True))
    return centered * lax.rsqrt(spread + epsilon) * gain_row + shift_row

def reference(tokens, ln_gain, ln_bias, w_qkv, b_qkv, w_out, b_out, merge_gain, merge_bias, segments, owners):
    normed = layer_norm(tokens.astype(jnp.float32), ln_gain, ln_bias).astype(jnp.bfloat16)
    projected = []
    for part_index in range(3):
        rows_out = jnp.dot(normed, w_qkv[part_index], preferred_element_type=jnp.float32) + b_qkv[part_index]
        projected.append(lax.optimization_barrier(rows_out.astype(jnp.bfloat16)))
    query, key_rows, value_rows = projected
    reach_rows = SPAN * TOK_DEV
    window_rows = 2 * reach_rows + TOK_DEV
    token_segment = jnp.repeat(segments, 4).astype(jnp.int32)
    padding = jnp.full((reach_rows,), -1, jnp.int32)
    padded_segment = jnp.concatenate([padding, token_segment, padding])
    padded_keys = jnp.pad(key_rows, ((reach_rows, reach_rows), (0, 0)))
    padded_values = jnp.pad(value_rows, ((reach_rows, reach_rows), (0, 0)))
    scale_factor = HEAD_DIM ** (-0.5)

    def one_block(block_index):
        row_start = (block_index * TOK_DEV).astype(jnp.int32)
        query_heads = lax.dynamic_slice_in_dim(query, row_start, TOK_DEV, 0).astype(jnp.float32).reshape(TOK_DEV, HEADS, HEAD_DIM)
        key_heads = lax.dynamic_slice_in_dim(padded_keys, row_start, window_rows, 0).astype(jnp.float32).reshape(window_rows, HEADS, HEAD_DIM)
        value_heads = lax.dynamic_slice_in_dim(padded_values, row_start, window_rows, 0).astype(jnp.float32).reshape(window_rows, HEADS, HEAD_DIM)
        query_segment = lax.dynamic_slice_in_dim(token_segment, row_start, TOK_DEV)
        key_segment = lax.dynamic_slice_in_dim(padded_segment, row_start, window_rows)
        scores = jnp.einsum('qhd,khd->hqk', query_heads, key_heads) * scale_factor
        allowed = query_segment[:, None] == key_segment[None, :]
        scores = jnp.where(allowed[None], scores, masked_score)
        row_top = lax.optimization_barrier(jnp.max(scores, axis=-1, keepdims=True))
        weights = jnp.exp(scores - row_top)
        totals = lax.optimization_barrier(jnp.sum(weights, axis=-1, keepdims=True))
        rounded = lax.optimization_barrier(weights.astype(jnp.bfloat16)).astype(jnp.float32)
        summed = jnp.einsum('hqk,khd->hqd', rounded, value_heads)
        return jnp.transpose(summed / totals, (1, 0, 2)).reshape(TOK_DEV, HEADS * HEAD_DIM).astype(jnp.bfloat16)
    attended = lax.map(one_block, jnp.arange(N_SEQ, dtype=jnp.int32)).reshape(TOKENS, D)
    group_width = D // N_TP
    head_total = jnp.zeros((TOKENS, D), jnp.float32)
    for group_index in range(N_TP):
        lower = group_index * group_width
        term = jnp.dot(attended[:, lower:lower + group_width], w_out[lower:lower + group_width], preferred_element_type=jnp.float32)
        head_total = head_total + lax.optimization_barrier(term.astype(jnp.bfloat16)).astype(jnp.float32)
    residual = tokens.astype(jnp.float32) + head_total + b_out
    merged = layer_norm(residual, merge_gain, merge_bias).astype(jnp.bfloat16).reshape(GROUPS, 4 * D)
    owner_rows = owners[:, 0].astype(jnp.int32).reshape(N_SEQ, MER_DEV)
    owner_table = (owner_rows[:, :, None] == jnp.arange(N_SEQ, dtype=jnp.int32)[None, None, :]).astype(jnp.int32)
    earlier = jnp.cumsum(owner_table, axis=1) - owner_table
    row_slot = lax.optimization_barrier(jnp.sum(earlier * owner_table, axis=2))
    source_index = jnp.arange(N_SEQ, dtype=jnp.int32)[:, None]
    target_row = (owner_rows * (N_SEQ * CAP) + source_index * CAP + row_slot).astype(jnp.int32).reshape(GROUPS)
    routed = jnp.zeros((N_SEQ * N_SEQ * CAP, 4 * D), jnp.bfloat16).at[target_row].set(merged)
    return routed
```

```python
import functools

import jax
import jax.numpy as jnp
from jax import lax
from jax.experimental import pallas as pl
from jax.experimental.pallas import tpu as pltpu
from jax.sharding import PartitionSpec as P

HEAD_DIM = 80
MESH = pl.DeviceIdType.MESH

epsilon = 1e-06
masked_score = -1e30


def layer_norm(values, gain_row, shift_row):
    center = jnp.mean(values, axis=-1, keepdims=True)
    centered = values - center
    spread = jnp.mean(centered * centered, axis=-1, keepdims=True)
    return centered * lax.rsqrt(spread + epsilon) * gain_row + shift_row


def iota(shape, dim):
    return lax.broadcasted_iota(jnp.int32, shape, dim)


def kernel(
    n_seq,
    n_tp,
    capacity,
    inside,
    tokens_ref,
    gain_ref,
    bias_ref,
    w_qkv_ref,
    b_qkv_ref,
    w_out_ref,
    b_out_ref,
    merge_gain_ref,
    merge_bias_ref,
    segments_ref,
    owners_ref,
    out_ref,
    kv,
    token_rows,
    normed_ref,
    query_ref,
    top_ref,
    total_ref,
    summed_ref,
    attended_ref,
    terms,
    arrived,
    outgoing,
    kv_send,
    kv_recv,
    tp_send,
    tp_recv,
    route_send,
    route_recv,
):
    tok_dev, model_width = tokens_ref.shape
    local_width = query_ref.shape[1]
    heads = local_width // HEAD_DIM
    quarter = tok_dev // n_tp
    n_pair = n_seq // 2
    me = lax.axis_index("seq")
    t_me = lax.axis_index("tp")
    pair = me // 2
    column = lax.rem(me, 2)
    partner = me + 1 - 2 * column
    has_low = pair > 0
    has_high = pair < n_pair - 1
    has_low2 = pair > 1
    has_high2 = pair < n_pair - 2

    barrier = pltpu.get_barrier_semaphore()
    for k in range(1, n_tp):
        pl.semaphore_signal(
            barrier, inc=1, device_id=(me, lax.rem(t_me + k, n_tp)), device_id_type=MESH
        )
    if inside:
        for k in range(1, n_seq):
            pl.semaphore_signal(
                barrier, inc=1, device_id=(lax.rem(me + k, n_seq), t_me), device_id_type=MESH
            )
    else:
        pl.semaphore_signal(barrier, inc=1, device_id=(partner, t_me), device_id_type=MESH)

        @pl.when(has_low)
        def _():
            pl.semaphore_signal(barrier, inc=1, device_id=(me - 2, t_me), device_id_type=MESH)

        @pl.when(has_high)
        def _():
            pl.semaphore_signal(barrier, inc=1, device_id=(me + 2, t_me), device_id_type=MESH)

    row = iota((tok_dev, tok_dev), 0)
    place = (lax.rem(row, quarter) * n_tp + row // quarter == iota((tok_dev, tok_dev), 1)).astype(
        jnp.bfloat16
    )
    ordered = jnp.dot(place, tokens_ref[...], preferred_element_type=jnp.float32)
    token_rows[...] = ordered.astype(jnp.bfloat16)
    normed_ref[...] = layer_norm(ordered, gain_ref[...], bias_ref[...]).astype(jnp.bfloat16)
    for i in (1, 2):
        kv[0, 2, :, (i - 1) * local_width : i * local_width] = (
            jnp.dot(normed_ref[...], w_qkv_ref[i], preferred_element_type=jnp.float32)
            + b_qkv_ref[i : i + 1, :]
        ).astype(jnp.bfloat16)

    if inside:
        pl.semaphore_wait(barrier, n_tp - 1 + n_seq - 1)
    else:
        pl.semaphore_wait(barrier, n_tp + has_low.astype(jnp.int32) + has_high.astype(jnp.int32))

    def hop(way, src, dst):
        target = (me - 2, me + 2, partner)[way]
        return pltpu.make_async_remote_copy(
            src_ref=kv.at[src[0], src[1]],
            dst_ref=kv.at[dst[0], dst[1]],
            send_sem=kv_send.at[way, src[0], src[1]],
            recv_sem=kv_recv.at[dst[0], dst[1]],
            device_id=(target, t_me),
            device_id_type=MESH,
        )

    low, high, across = 0, 1, 2
    sends = {
        "own": [
            (low, (0, 2), (0, 3), has_low),
            (high, (0, 2), (0, 1), has_high),
            (across, (0, 2), (1, 2), None),
        ],
        "partner": [
            (high, (1, 2), (1, 1), pair == 0),
            (low, (1, 2), (1, 3), pair == n_pair - 1),
        ],
        "low": [
            (high, (0, 1), (0, 0), has_low & has_high),
            (across, (0, 1), (1, 1), has_low & (pair != 1)),
        ],
        "high": [
            (low, (0, 3), (0, 4), has_low & has_high),
            (across, (0, 3), (1, 3), has_high & (pair != n_pair - 2)),
        ],
        "low2": [(across, (0, 0), (1, 0), has_low2 & (column == 1))],
        "high2": [(across, (0, 4), (1, 4), has_high2 & (column == 0))],
    }

    def guarded(condition, action):
        if condition is None:
            action()
        else:
            pl.when(condition)(action)

    def send(name):
        for way, src, dst, condition in sends[name]:
            guarded(condition, lambda: hop(way, src, dst).start())

    def landed(slot, condition):
        def wait():
            hop(across, slot, slot).wait_recv()

        guarded(condition, wait)

    send("own")
    query_ref[...] = (
        jnp.dot(normed_ref[...], w_qkv_ref[0], preferred_element_type=jnp.float32)
        + b_qkv_ref[0:1, :]
    ).astype(jnp.bfloat16)

    def segment_row(block):
        return jnp.concatenate([segments_ref[block]] * n_tp, axis=1)

    scale_factor = HEAD_DIM ** (-0.5)
    own_row = segment_row(me)
    eye = row == iota((tok_dev, tok_dev), 1)
    own_segment = jnp.sum(jnp.where(eye, own_row, 0), axis=1, keepdims=True)

    def absorb(slot, block, first=False):
        allowed = own_segment == segment_row(block)
        for h in range(heads):
            lanes = slice(h * HEAD_DIM, (h + 1) * HEAD_DIM)
            keys = kv[slot[0], slot[1], :, lanes]
            values = kv[
                slot[0], slot[1], :, local_width + h * HEAD_DIM : local_width + (h + 1) * HEAD_DIM
            ]
            scores = (
                lax.dot_general(
                    query_ref[:, lanes],
                    keys,
                    (((1,), (1,)), ((), ())),
                    preferred_element_type=jnp.float32,
                )
                * scale_factor
            )
            scores = jnp.where(allowed, scores, masked_score)
            top = jnp.max(scores, axis=1, keepdims=True)
            if not first:
                old = top_ref[h]
                top = jnp.maximum(old, top)
            weights = jnp.exp(scores - top)
            total = jnp.sum(weights, axis=1, keepdims=True)
            summed = jnp.dot(
                weights.astype(jnp.bfloat16), values, preferred_element_type=jnp.float32
            )
            if not first:
                factor = jnp.exp(old - top)
                total = total_ref[h] * factor + total
                summed = summed_ref[h] * factor + summed
            top_ref[h] = top
            total_ref[h] = total
            summed_ref[h] = summed

    def absorb_if(slot, condition):
        block = 2 * (pair + slot[1] - 2) + (column if slot[0] == 0 else 1 - column)
        guarded(condition, lambda: absorb(slot, block))

    absorb((0, 2), me, first=True)
    landed((1, 2), None)
    send("partner")
    landed((0, 1), has_low)
    send("low")
    landed((0, 3), has_high)
    send("high")
    absorb_if((1, 2), None)
    absorb_if((0, 1), has_low)
    absorb_if((0, 3), has_high)
    landed((0, 0), has_low2)
    send("low2")
    landed((0, 4), has_high2)
    send("high2")
    absorb_if((0, 0), has_low2)
    absorb_if((0, 4), has_high2)
    landed((1, 1), has_low)
    absorb_if((1, 1), has_low)
    landed((1, 3), has_high)
    absorb_if((1, 3), has_high)
    far_low = has_low2 & (column == 0)
    far_high = has_high2 & (column == 1)
    landed((1, 0), far_low)
    absorb_if((1, 0), far_low)
    landed((1, 4), far_high)
    absorb_if((1, 4), far_high)

    for h in range(heads):
        attended_ref[:, h * HEAD_DIM : (h + 1) * HEAD_DIM] = (
            summed_ref[h] / total_ref[h]
        ).astype(jnp.bfloat16)

    def tp_copy(k):
        target = lax.rem(t_me + k, n_tp)
        return pltpu.make_async_remote_copy(
            src_ref=terms.at[target],
            dst_ref=arrived.at[k],
            send_sem=tp_send.at[k],
            recv_sem=tp_recv.at[k],
            device_id=(me, target),
            device_id_type=MESH,
        )

    for k in (2, 3, 1, 0):
        target = lax.rem(t_me + k, n_tp)
        rows = attended_ref[pl.ds(pl.multiple_of(target * quarter, quarter), quarter), :]
        terms[target] = jnp.dot(
            rows, w_out_ref[...], preferred_element_type=jnp.float32
        ).astype(jnp.bfloat16)
        if k:
            tp_copy(k).start()

    lanes = max(n_seq, 128)
    owner = owners_ref[...]
    table = (owner == iota((quarter, lanes), 1)).astype(jnp.float32)
    before = (iota((quarter, quarter), 1) < iota((quarter, quarter), 0)).astype(jnp.bfloat16)
    earlier = jnp.dot(before, table.astype(jnp.bfloat16), preferred_element_type=jnp.float32)
    slot = jnp.sum(earlier * table, axis=1, keepdims=True).astype(jnp.int32)
    goal = owner * capacity + slot
    placing = (goal == iota((quarter, n_seq * capacity), 1)).astype(jnp.bfloat16)

    residual = token_rows[
        pl.ds(pl.multiple_of(t_me * quarter, quarter), quarter), :
    ].astype(jnp.float32)
    head_total = terms[t_me].astype(jnp.float32)
    for k in (1, 3, 2):
        tp_copy(k).wait_recv()
        head_total = head_total + arrived[k].astype(jnp.float32)
    residual = residual + head_total + b_out_ref[...]
    merged = layer_norm(residual, merge_gain_ref[...], merge_bias_ref[...]).astype(jnp.bfloat16)
    placed = lax.dot_general(
        placing, merged, (((0,), (0,)), ((), ())), preferred_element_type=jnp.float32
    ).astype(jnp.bfloat16)

    if inside:
        outgoing[...] = placed.reshape(n_seq, capacity, model_width)

        def route(k):
            target = lax.rem(me + k, n_seq)
            return pltpu.make_async_remote_copy(
                src_ref=outgoing.at[target],
                dst_ref=out_ref.at[me],
                send_sem=route_send.at[k],
                recv_sem=route_recv.at[k],
                device_id=(target, t_me),
                device_id_type=MESH,
            )

        def route_in(k):
            source = lax.rem(me + n_seq - k, n_seq)
            return pltpu.make_async_remote_copy(
                src_ref=outgoing.at[source],
                dst_ref=out_ref.at[source],
                send_sem=route_send.at[k],
                recv_sem=route_recv.at[k],
                device_id=(source, t_me),
                device_id_type=MESH,
            )

        order = sorted(range(1, n_seq), key=lambda k: -abs(n_seq // 2 - k))[::-1]
        for k in order:
            route(k).start()
        out_ref[me] = outgoing[me]
    else:
        out_ref[...] = placed

    for name in sends:
        for way, src, dst, condition in sends[name]:
            guarded(condition, lambda: hop(way, src, dst).wait_send())
    for k in range(1, n_tp):
        tp_copy(k).wait_send()
    if inside:
        for k in order:
            route_in(k).wait_recv()
        for k in order:
            route(k).wait_send()


def per_device(
    tokens, ln_gain, ln_bias, w_qkv, b_qkv, w_out, b_out, merge_gain, merge_bias, segments, owners
):
    tok_dev, model_width = tokens.shape
    local_width = w_qkv.shape[2]
    heads = local_width // HEAD_DIM
    n_seq = lax.axis_size("seq")
    n_tp = lax.axis_size("tp")
    quarter = tok_dev // n_tp
    capacity = max(2, 2 * quarter // n_seq)
    inside = capacity % 16 == 0
    out_shape = (n_seq, capacity, model_width) if inside else (n_seq * capacity, model_width)
    vmem = pl.BlockSpec(memory_space=pltpu.VMEM)
    routed = pl.pallas_call(
        functools.partial(kernel, n_seq, n_tp, capacity, inside),
        out_shape=jax.ShapeDtypeStruct(out_shape, jnp.bfloat16),
        in_specs=[vmem] * 11,
        out_specs=vmem,
        scratch_shapes=[
            pltpu.VMEM((2, 5, tok_dev, 2 * local_width), jnp.bfloat16),
            pltpu.VMEM((tok_dev, model_width), jnp.bfloat16),
            pltpu.VMEM((tok_dev, model_width), jnp.bfloat16),
            pltpu.VMEM((tok_dev, local_width), jnp.bfloat16),
            pltpu.VMEM((heads, tok_dev, 1), jnp.float32),
            pltpu.VMEM((heads, tok_dev, 1), jnp.float32),
            pltpu.VMEM((heads, tok_dev, HEAD_DIM), jnp.float32),
            pltpu.VMEM((tok_dev, local_width), jnp.bfloat16),
            pltpu.VMEM((n_tp, quarter, model_width), jnp.bfloat16),
            pltpu.VMEM((n_tp, quarter, model_width), jnp.bfloat16),
            pltpu.VMEM((n_seq, max(capacity, 16), model_width) if inside else (1, 16, 128), jnp.bfloat16),
            pltpu.SemaphoreType.DMA((3, 2, 5)),
            pltpu.SemaphoreType.DMA((2, 5)),
            pltpu.SemaphoreType.DMA((n_tp,)),
            pltpu.SemaphoreType.DMA((n_tp,)),
            pltpu.SemaphoreType.DMA((n_seq,)),
            pltpu.SemaphoreType.DMA((n_seq,)),
        ],
        compiler_params=pltpu.CompilerParams(
            collective_id=0, has_side_effects=True, vmem_limit_bytes=48 * 1024 * 1024
        ),
        cost_estimate=pl.CostEstimate(
            flops=2 * 10**9, bytes_accessed=5 * 10**6, transcendentals=3 * 10**6
        ),
    )(
        tokens,
        ln_gain[None, :],
        ln_bias[None, :],
        w_qkv,
        b_qkv,
        w_out,
        b_out[None, :],
        merge_gain[None, :],
        merge_bias[None, :],
        segments.reshape(n_seq, 1, quarter),
        owners,
    )
    if inside:
        return routed.reshape(n_seq * capacity, model_width)
    return lax.all_to_all(routed, "seq", split_axis=0, concat_axis=0, tiled=True)


def solution(mesh):
    placed = (
        P("seq", None),
        P(),
        P(),
        P(None, None, "tp"),
        P(None, "tp"),
        P("tp", None),
        P(),
        P(),
        P(),
        P(),
        P("seq", None),
    )
    return jax.shard_map(
        per_device, mesh=mesh, in_specs=placed, out_specs=P("seq", "tp"), check_vma=False
    )
```

```python
import functools
import math

import jax
import jax.numpy as jnp
from jax import lax
from jax.experimental import pallas as pl
from jax.experimental.pallas import tpu as pltpu
from jax.sharding import PartitionSpec as P

HEAD_DIM = 80
MESH = pl.DeviceIdType.MESH

epsilon = 1e-06
masked_score = -1e30


def layer_norm(values, gain_row, shift_row):
    center = jnp.mean(values, axis=-1, keepdims=True)
    centered = values - center
    spread = jnp.mean(centered * centered, axis=-1, keepdims=True)
    return centered * lax.rsqrt(spread + epsilon) * gain_row + shift_row


def row_of(ref):
    return ref[...].reshape(1, ref.shape[0])


def iota(shape, dim):
    return lax.broadcasted_iota(jnp.int32, shape, dim)


def kernel(
    n_seq,
    n_tp,
    capacity,
    inside,
    tokens_hbm,
    gain_ref,
    bias_ref,
    w_qkv_hbm,
    b_qkv_ref,
    w_out_hbm,
    b_out_ref,
    merge_gain_ref,
    merge_bias_ref,
    segments_ref,
    owners_ref,
    out_ref,
    tokens_ref,
    w_qkv_ref,
    w_out_ref,
    segment_rows,
    kv,
    token_rows,
    normed_ref,
    query_ref,
    top_ref,
    total_ref,
    summed_ref,
    attended_ref,
    terms,
    arrived,
    pair_sum,
    outgoing,
    load_sem,
    kv_send,
    kv_recv,
    tp_send,
    tp_recv,
    route_send,
    route_recv,
):
    tok_dev, model_width = tokens_ref.shape
    local_width = query_ref.shape[1]
    heads = local_width // HEAD_DIM
    quarter = tok_dev // n_tp
    n_pair = n_seq // 2
    me = lax.axis_index("seq")
    t_me = lax.axis_index("tp")
    pair = me // 2
    column = lax.rem(me, 2)
    partner = me + 1 - 2 * column
    has_low = pair > 0
    has_high = pair < n_pair - 1
    has_low2 = pair > 1
    has_high2 = pair < n_pair - 2

    loads = [
        pltpu.make_async_copy(tokens_hbm, tokens_ref, load_sem.at[0]),
        pltpu.make_async_copy(w_qkv_hbm.at[1], w_qkv_ref.at[1], load_sem.at[1]),
        pltpu.make_async_copy(w_qkv_hbm.at[2], w_qkv_ref.at[2], load_sem.at[2]),
        pltpu.make_async_copy(w_qkv_hbm.at[0], w_qkv_ref.at[0], load_sem.at[3]),
        pltpu.make_async_copy(w_out_hbm, w_out_ref, load_sem.at[4]),
    ]
    for load in loads:
        load.start()

    barrier = pltpu.get_barrier_semaphore()
    for k in range(1, n_tp):
        pl.semaphore_signal(
            barrier, inc=1, device_id=(me, lax.rem(t_me + k, n_tp)), device_id_type=MESH
        )
    if inside:
        for k in range(1, n_seq):
            pl.semaphore_signal(
                barrier, inc=1, device_id=(lax.rem(me + k, n_seq), t_me), device_id_type=MESH
            )
    else:
        pl.semaphore_signal(barrier, inc=1, device_id=(partner, t_me), device_id_type=MESH)

        @pl.when(has_low)
        def _():
            pl.semaphore_signal(barrier, inc=1, device_id=(me - 2, t_me), device_id_type=MESH)

        @pl.when(has_high)
        def _():
            pl.semaphore_signal(barrier, inc=1, device_id=(me + 2, t_me), device_id_type=MESH)

    row = iota((tok_dev, tok_dev), 0)
    place = (lax.rem(row, quarter) * n_tp + row // quarter == iota((tok_dev, tok_dev), 1)).astype(
        jnp.bfloat16
    )
    loads[0].wait()
    ordered = jnp.dot(place, tokens_ref[...], preferred_element_type=jnp.float32)
    token_rows[...] = ordered.astype(jnp.bfloat16)
    normed_ref[...] = layer_norm(ordered, row_of(gain_ref), row_of(bias_ref)).astype(jnp.bfloat16)

    def project(i):
        return (
            lax.dot_general(
                normed_ref[...],
                w_qkv_ref[i],
                (((1,), (1,)), ((), ())),
                preferred_element_type=jnp.float32,
            )
            + b_qkv_ref[i : i + 1, :]
        ).astype(jnp.bfloat16)

    loads[1].wait()
    kv[0, 2, 0] = project(1)

    if inside:
        pl.semaphore_wait(barrier, n_tp - 1 + n_seq - 1)
    else:
        pl.semaphore_wait(barrier, n_tp + has_low.astype(jnp.int32) + has_high.astype(jnp.int32))

    def hop(way, src, dst, half):
        target = (me - 2, me + 2, partner)[way]
        return pltpu.make_async_remote_copy(
            src_ref=kv.at[src[0], src[1], half],
            dst_ref=kv.at[dst[0], dst[1], half],
            send_sem=kv_send.at[way, src[0], src[1], half],
            recv_sem=kv_recv.at[dst[0], dst[1], half],
            device_id=(target, t_me),
            device_id_type=MESH,
        )

    low, high, across = 0, 1, 2
    at_first = pair == 0
    at_last = pair == n_pair - 1
    sends = {
        "own": [
            (low, (0, 2), (0, 3), has_low, has_low),
            (high, (0, 2), (0, 1), has_high, has_high),
            (across, (0, 2), (1, 2), None, None),
        ],
        "partner": [
            (high, (1, 2), (1, 1), at_first, at_first | (has_high & (column == 0))),
            (low, (1, 2), (1, 3), at_last, at_last | (has_low & (column == 1))),
        ],
        "low": [
            (high, (0, 1), (0, 0), has_low & has_high, has_low & has_high),
            (
                across,
                (0, 1),
                (1, 1),
                has_low & (pair != 1),
                has_low & (pair != 1) & (column == 0),
            ),
        ],
        "high": [
            (low, (0, 3), (0, 4), has_low & has_high, has_low & has_high),
            (
                across,
                (0, 3),
                (1, 3),
                has_high & (pair != n_pair - 2),
                has_high & (pair != n_pair - 2) & (column == 1),
            ),
        ],
        "low2": [
            (across, (0, 0), (1, 0), has_low2 & (column == 1), has_low2 & (column == 1))
        ],
        "high2": [
            (across, (0, 4), (1, 4), has_high2 & (column == 0), has_high2 & (column == 0))
        ],
    }

    def guarded(condition, action):
        if condition is None:
            action()
        else:
            pl.when(condition)(action)

    def send(name, half):
        for way, src, dst, *conditions in sends[name]:
            guarded(conditions[half], lambda: hop(way, src, dst, half).start())

    def landed(slot, half, condition):
        guarded(condition, lambda: hop(across, slot, slot, half).wait_recv())

    send("own", 0)
    loads[2].wait()
    kv[0, 2, 1] = project(2)
    send("own", 1)
    loads[3].wait()
    query_ref[...] = project(0)

    segments = row_of(segments_ref)
    for block in range(n_seq):
        segment_rows[block] = jnp.concatenate(
            [segments[:, block * quarter : (block + 1) * quarter]] * n_tp, axis=1
        )

    def segment_row(block):
        return segment_rows[block]

    exponent_scale = HEAD_DIM ** (-0.5) * math.log2(math.e)
    own_row = segment_row(me)
    eye = row == iota((tok_dev, tok_dev), 1)
    own_segment = jnp.sum(jnp.where(eye, own_row, 0), axis=1, keepdims=True)

    def absorb(slot, block, first=False):
        allowed = own_segment == segment_row(block)
        for h in range(heads):
            lanes = slice(h * HEAD_DIM, (h + 1) * HEAD_DIM)
            keys = kv[slot[0], slot[1], 0, :, lanes]
            values = kv[slot[0], slot[1], 1, :, lanes]
            scores = lax.dot_general(
                query_ref[:, lanes],
                keys,
                (((1,), (1,)), ((), ())),
                preferred_element_type=jnp.float32,
            )
            scores = jnp.where(allowed, scores, masked_score)
            top = jnp.max(scores, axis=1, keepdims=True)
            if not first:
                old = top_ref[h]
                top = jnp.maximum(old, top)
            weights = jnp.exp2((scores - top) * exponent_scale)
            total = jnp.sum(weights, axis=1, keepdims=True)
            summed = jnp.dot(
                weights.astype(jnp.bfloat16), values, preferred_element_type=jnp.float32
            )
            if not first:
                factor = jnp.exp2((old - top) * exponent_scale)
                total = total_ref[h] * factor + total
                summed = summed_ref[h] * factor + summed
            top_ref[h] = top
            total_ref[h] = total
            summed_ref[h] = summed

    def absorb_if(slot, condition):
        block = 2 * (pair + slot[1] - 2) + (column if slot[0] == 0 else 1 - column)
        guarded(condition, lambda: absorb(slot, block))

    absorb((0, 2), me, first=True)
    for half in (0, 1):
        landed((0, 1), half, has_low)
        send("low", half)
        landed((0, 3), half, has_high)
        send("high", half)
        landed((1, 2), half, None)
        send("partner", half)
    absorb_if((1, 2), None)
    absorb_if((0, 1), has_low)
    absorb_if((0, 3), has_high)
    for half in (0, 1):
        landed((0, 0), half, has_low2)
        send("low2", half)
        landed((0, 4), half, has_high2)
        send("high2", half)
    absorb_if((0, 0), has_low2)
    absorb_if((0, 4), has_high2)
    far_low = has_low2 & (column == 0)
    far_high = has_high2 & (column == 1)
    for slot, condition in (
        ((1, 1), has_low),
        ((1, 3), has_high),
        ((1, 0), far_low),
        ((1, 4), far_high),
    ):
        for half in (0, 1):
            landed(slot, half, condition)
        absorb_if(slot, condition)

    for h in range(heads):
        attended_ref[:, h * HEAD_DIM : (h + 1) * HEAD_DIM] = (
            summed_ref[h] / total_ref[h]
        ).astype(jnp.bfloat16)

    opposite = lax.rem(t_me + n_tp // 2, n_tp)
    sibling = t_me + 1 - 2 * lax.rem(t_me, 2)
    diagonal = lax.rem(sibling + n_tp // 2, n_tp)

    def tp_copy(k):
        return pltpu.make_async_remote_copy(
            src_ref=(terms.at[diagonal], terms.at[sibling], pair_sum)[k],
            dst_ref=arrived.at[k],
            send_sem=tp_send.at[k],
            recv_sem=tp_recv.at[k],
            device_id=(me, (sibling, sibling, opposite)[k]),
            device_id_type=MESH,
        )

    loads[4].wait()

    def term(target):
        rows = attended_ref[pl.ds(pl.multiple_of(target * quarter, quarter), quarter), :]
        terms[target] = jnp.dot(
            rows, w_out_ref[...], preferred_element_type=jnp.float32
        ).astype(jnp.bfloat16)

    term(diagonal)
    tp_copy(0).start()
    term(opposite)
    tp_copy(0).wait_recv()
    pair_sum[...] = (
        terms[opposite].astype(jnp.float32) + arrived[0].astype(jnp.float32)
    ).astype(jnp.bfloat16)
    tp_copy(2).start()
    term(sibling)
    tp_copy(1).start()
    term(t_me)

    lanes = max(n_seq, 128)
    own_lane = iota((quarter, quarter), 0) == iota((quarter, quarter), 1)
    owner = jnp.sum(jnp.where(own_lane, owners_ref[...], 0), axis=1, keepdims=True)
    table = (owner == iota((quarter, lanes), 1)).astype(jnp.float32)
    before = (iota((quarter, quarter), 1) < iota((quarter, quarter), 0)).astype(jnp.bfloat16)
    earlier = jnp.dot(before, table.astype(jnp.bfloat16), preferred_element_type=jnp.float32)
    slot = jnp.sum(earlier * table, axis=1, keepdims=True).astype(jnp.int32)
    goal = owner * capacity + slot
    placing = (goal == iota((quarter, n_seq * capacity), 1)).astype(jnp.bfloat16)

    residual = token_rows[
        pl.ds(pl.multiple_of(t_me * quarter, quarter), quarter), :
    ].astype(jnp.float32)
    head_total = terms[t_me].astype(jnp.float32)
    for k in (1, 2):
        tp_copy(k).wait_recv()
        head_total = head_total + arrived[k].astype(jnp.float32)
    residual = residual + head_total + row_of(b_out_ref)
    merged = layer_norm(residual, row_of(merge_gain_ref), row_of(merge_bias_ref)).astype(jnp.bfloat16)
    placed = lax.dot_general(
        placing, merged, (((0,), (0,)), ((), ())), preferred_element_type=jnp.float32
    ).astype(jnp.bfloat16)

    if inside:
        outgoing[...] = placed.reshape(n_seq, capacity, model_width)

        def route(k):
            target = lax.rem(me + k, n_seq)
            return pltpu.make_async_remote_copy(
                src_ref=outgoing.at[target],
                dst_ref=out_ref.at[me],
                send_sem=route_send.at[k],
                recv_sem=route_recv.at[k],
                device_id=(target, t_me),
                device_id_type=MESH,
            )

        def route_in(k):
            source = lax.rem(me + n_seq - k, n_seq)
            return pltpu.make_async_remote_copy(
                src_ref=outgoing.at[source],
                dst_ref=out_ref.at[source],
                send_sem=route_send.at[k],
                recv_sem=route_recv.at[k],
                device_id=(source, t_me),
                device_id_type=MESH,
            )

        order = sorted(range(1, n_seq), key=lambda k: -abs(n_seq // 2 - k))[::-1]
        for k in order:
            route(k).start()
        out_ref[me] = outgoing[me]
    else:
        out_ref[...] = placed

    for name in sends:
        for way, src, dst, *conditions in sends[name]:
            for half in (0, 1):
                guarded(conditions[half], lambda: hop(way, src, dst, half).wait_send())
    for k in range(3):
        tp_copy(k).wait_send()
    if inside:
        for k in order:
            route_in(k).wait_recv()
        for k in order:
            route(k).wait_send()


def per_device(
    tokens, ln_gain, ln_bias, w_qkv, b_qkv, w_out, b_out, merge_gain, merge_bias, segments, owners
):
    tok_dev, model_width = tokens.shape
    local_width = w_qkv.shape[2]
    heads = local_width // HEAD_DIM
    n_seq = lax.axis_size("seq")
    n_tp = lax.axis_size("tp")
    quarter = tok_dev // n_tp
    capacity = max(2, 2 * quarter // n_seq)
    inside = capacity % 16 == 0
    out_shape = (n_seq, capacity, model_width) if inside else (n_seq * capacity, model_width)
    vmem = pl.BlockSpec(memory_space=pltpu.VMEM)
    hbm = pl.BlockSpec(memory_space=pltpu.HBM)
    routed = pl.pallas_call(
        functools.partial(kernel, n_seq, n_tp, capacity, inside),
        out_shape=jax.ShapeDtypeStruct(out_shape, jnp.bfloat16),
        in_specs=[hbm, vmem, vmem, hbm, vmem, hbm] + [vmem] * 5,
        out_specs=vmem,
        scratch_shapes=[
            pltpu.VMEM((tok_dev, model_width), jnp.bfloat16),
            pltpu.VMEM((3, local_width, model_width), jnp.bfloat16),
            pltpu.VMEM((local_width, model_width), jnp.bfloat16),
            pltpu.VMEM((n_seq, 1, tok_dev), jnp.int32),
            pltpu.VMEM((2, 5, 2, tok_dev, local_width), jnp.bfloat16),
            pltpu.VMEM((tok_dev, model_width), jnp.bfloat16),
            pltpu.VMEM((tok_dev, model_width), jnp.bfloat16),
            pltpu.VMEM((tok_dev, local_width), jnp.bfloat16),
            pltpu.VMEM((heads, tok_dev, 1), jnp.float32),
            pltpu.VMEM((heads, tok_dev, 1), jnp.float32),
            pltpu.VMEM((heads, tok_dev, HEAD_DIM), jnp.float32),
            pltpu.VMEM((tok_dev, local_width), jnp.bfloat16),
            pltpu.VMEM((n_tp, quarter, model_width), jnp.bfloat16),
            pltpu.VMEM((3, quarter, model_width), jnp.bfloat16),
            pltpu.VMEM((quarter, model_width), jnp.bfloat16),
            pltpu.VMEM((n_seq, max(capacity, 16), model_width) if inside else (1, 16, 128), jnp.bfloat16),
            pltpu.SemaphoreType.DMA((5,)),
            pltpu.SemaphoreType.DMA((3, 2, 5, 2)),
            pltpu.SemaphoreType.DMA((2, 5, 2)),
            pltpu.SemaphoreType.DMA((3,)),
            pltpu.SemaphoreType.DMA((3,)),
            pltpu.SemaphoreType.DMA((n_seq,)),
            pltpu.SemaphoreType.DMA((n_seq,)),
        ],
        compiler_params=pltpu.CompilerParams(
            collective_id=0, has_side_effects=True, vmem_limit_bytes=60 * 1024 * 1024
        ),
        cost_estimate=pl.CostEstimate(
            flops=2 * 10**9, bytes_accessed=5 * 10**6, transcendentals=3 * 10**6
        ),
    )(
        tokens,
        ln_gain,
        ln_bias,
        jnp.swapaxes(w_qkv, 1, 2),
        b_qkv,
        w_out,
        b_out,
        merge_gain,
        merge_bias,
        segments,
        owners.T,
    )
    if inside:
        return routed.reshape(n_seq * capacity, model_width)
    return lax.all_to_all(routed, "seq", split_axis=0, concat_axis=0, tiled=True)


def solution(mesh):
    placed = (
        P("seq", None),
        P(),
        P(),
        P(None, None, "tp"),
        P(None, "tp"),
        P("tp", None),
        P(),
        P(),
        P(),
        P(),
        P("seq", None),
    )
    return jax.shard_map(
        per_device, mesh=mesh, in_specs=placed, out_specs=P("seq", "tp"), check_vma=False
    )
```

```python
import functools
import math

import jax
import jax.numpy as jnp
from jax import lax
from jax.experimental import pallas as pl
from jax.experimental.pallas import tpu as pltpu
from jax.sharding import PartitionSpec as P

HEAD_DIM = 80
MESH = pl.DeviceIdType.MESH

epsilon = 1e-06
masked_score = -1e30


def layer_norm(values, gain_row, shift_row):
    center = jnp.mean(values, axis=-1, keepdims=True)
    centered = values - center
    spread = jnp.mean(centered * centered, axis=-1, keepdims=True)
    return centered * lax.rsqrt(spread + epsilon) * gain_row + shift_row


def row_of(ref):
    return ref[...].reshape(1, ref.shape[0])


def iota(shape, dim):
    return lax.broadcasted_iota(jnp.int32, shape, dim)


def kernel(
    n_seq,
    n_tp,
    capacity,
    inside,
    tokens_hbm,
    gain_ref,
    bias_ref,
    w_qkv_hbm,
    b_qkv_ref,
    w_out_hbm,
    b_out_ref,
    merge_gain_ref,
    merge_bias_ref,
    segments_ref,
    owners_ref,
    out_ref,
    tokens_ref,
    w_qkv_ref,
    w_out_ref,
    segment_rows,
    kv,
    token_rows,
    normed_ref,
    query_ref,
    top_ref,
    total_ref,
    summed_ref,
    attended_ref,
    terms,
    arrived,
    pair_sum,
    outgoing,
    load_sem,
    kv_send,
    kv_recv,
    tp_send,
    tp_recv,
    route_send,
    route_recv,
):
    tok_dev, model_width = tokens_ref.shape
    local_width = query_ref.shape[1]
    heads = local_width // HEAD_DIM
    quarter = tok_dev // n_tp
    n_pair = n_seq // 2
    me = lax.axis_index("seq")
    t_me = lax.axis_index("tp")
    pair = me // 2
    column = lax.rem(me, 2)
    partner = me + 1 - 2 * column
    has_low = pair > 0
    has_high = pair < n_pair - 1
    has_low2 = pair > 1
    has_high2 = pair < n_pair - 2

    loads = [
        pltpu.make_async_copy(tokens_hbm, tokens_ref, load_sem.at[0]),
        pltpu.make_async_copy(w_qkv_hbm.at[1], w_qkv_ref.at[1], load_sem.at[1]),
        pltpu.make_async_copy(w_qkv_hbm.at[2], w_qkv_ref.at[2], load_sem.at[2]),
        pltpu.make_async_copy(w_qkv_hbm.at[0], w_qkv_ref.at[0], load_sem.at[3]),
        pltpu.make_async_copy(w_out_hbm, w_out_ref, load_sem.at[4]),
    ]
    for load in loads:
        load.start()

    barrier = pltpu.get_barrier_semaphore()
    for k in range(1, n_tp):
        pl.semaphore_signal(
            barrier, inc=1, device_id=(me, lax.rem(t_me + k, n_tp)), device_id_type=MESH
        )
    if inside:
        for k in range(1, n_seq):
            pl.semaphore_signal(
                barrier, inc=1, device_id=(lax.rem(me + k, n_seq), t_me), device_id_type=MESH
            )
    else:
        pl.semaphore_signal(barrier, inc=1, device_id=(partner, t_me), device_id_type=MESH)

        @pl.when(has_low)
        def _():
            pl.semaphore_signal(barrier, inc=1, device_id=(me - 2, t_me), device_id_type=MESH)

        @pl.when(has_high)
        def _():
            pl.semaphore_signal(barrier, inc=1, device_id=(me + 2, t_me), device_id_type=MESH)

    row = iota((tok_dev, tok_dev), 0)
    place = (lax.rem(row, quarter) * n_tp + row // quarter == iota((tok_dev, tok_dev), 1)).astype(
        jnp.bfloat16
    )
    loads[0].wait()
    ordered = jnp.dot(place, tokens_ref[...], preferred_element_type=jnp.float32)
    token_rows[...] = ordered.astype(jnp.bfloat16)
    normed_ref[...] = layer_norm(ordered, row_of(gain_ref), row_of(bias_ref)).astype(jnp.bfloat16)

    def project(i):
        return (
            lax.dot_general(
                normed_ref[...],
                w_qkv_ref[i],
                (((1,), (1,)), ((), ())),
                preferred_element_type=jnp.float32,
            )
            + b_qkv_ref[i : i + 1, :]
        ).astype(jnp.bfloat16)

    loads[1].wait()
    kv[0, 2, 0] = project(1)

    if inside:
        pl.semaphore_wait(barrier, n_tp - 1 + n_seq - 1)
    else:
        pl.semaphore_wait(barrier, n_tp + has_low.astype(jnp.int32) + has_high.astype(jnp.int32))

    def hop(way, src, dst, half):
        target = (me - 2, me + 2, partner)[way]
        return pltpu.make_async_remote_copy(
            src_ref=kv.at[src[0], src[1], half],
            dst_ref=kv.at[dst[0], dst[1], half],
            send_sem=kv_send.at[way, src[0], src[1], half],
            recv_sem=kv_recv.at[dst[0], dst[1], half],
            device_id=(target, t_me),
            device_id_type=MESH,
        )

    low, high, across = 0, 1, 2
    at_first = pair == 0
    at_last = pair == n_pair - 1
    sends = {
        "own": [
            (low, (0, 2), (0, 3), has_low, has_low),
            (high, (0, 2), (0, 1), has_high, has_high),
            (across, (0, 2), (1, 2), None, None),
        ],
        "partner": [
            (high, (1, 2), (1, 1), at_first, at_first | (has_high & (column == 0))),
            (low, (1, 2), (1, 3), at_last, at_last | (has_low & (column == 1))),
        ],
        "low": [
            (high, (0, 1), (0, 0), has_low & has_high, has_low & has_high),
            (
                across,
                (0, 1),
                (1, 1),
                has_low & (pair != 1),
                has_low & (pair != 1) & (column == 0),
            ),
        ],
        "high": [
            (low, (0, 3), (0, 4), has_low & has_high, has_low & has_high),
            (
                across,
                (0, 3),
                (1, 3),
                has_high & (pair != n_pair - 2),
                has_high & (pair != n_pair - 2) & (column == 1),
            ),
        ],
        "low2": [
            (across, (0, 0), (1, 0), has_low2 & (column == 1), has_low2 & (column == 1))
        ],
        "high2": [
            (across, (0, 4), (1, 4), has_high2 & (column == 0), has_high2 & (column == 0))
        ],
    }

    def guarded(condition, action):
        if condition is None:
            action()
        else:
            pl.when(condition)(action)

    def send(name, half):
        for way, src, dst, *conditions in sends[name]:
            guarded(conditions[half], lambda: hop(way, src, dst, half).start())

    def landed(slot, half, condition):
        guarded(condition, lambda: hop(across, slot, slot, half).wait_recv())

    send("own", 0)
    loads[2].wait()
    kv[0, 2, 1] = project(2)
    send("own", 1)
    loads[3].wait()
    query_ref[...] = project(0)

    segments = row_of(segments_ref)
    for block in range(n_seq):
        segment_rows[block] = jnp.concatenate(
            [segments[:, block * quarter : (block + 1) * quarter]] * n_tp, axis=1
        )

    def segment_row(block):
        return segment_rows[block]

    exponent_scale = HEAD_DIM ** (-0.5) * math.log2(math.e)
    own_row = segment_row(me)
    eye = row == iota((tok_dev, tok_dev), 1)
    own_segment = jnp.sum(jnp.where(eye, own_row, 0), axis=1, keepdims=True)

    def block_of(slot):
        return 2 * (pair + slot[1] - 2) + (column if slot[0] == 0 else 1 - column)

    def absorb(slots, first=False):
        allowed = [own_segment == segment_row(block_of(slot)) for slot in slots]
        for h in range(heads):
            lanes = slice(h * HEAD_DIM, (h + 1) * HEAD_DIM)
            query = query_ref[:, lanes]
            scores = [
                jnp.where(
                    mask,
                    lax.dot_general(
                        query,
                        kv[slot[0], slot[1], 0, :, lanes],
                        (((1,), (1,)), ((), ())),
                        preferred_element_type=jnp.float32,
                    ),
                    masked_score,
                )
                for slot, mask in zip(slots, allowed)
            ]
            top = jnp.max(functools.reduce(jnp.maximum, scores), axis=1, keepdims=True)
            if not first:
                old = top_ref[h]
                top = jnp.maximum(old, top)
            weights = [jnp.exp2((part - top) * exponent_scale) for part in scores]
            total = jnp.sum(functools.reduce(jnp.add, weights), axis=1, keepdims=True)
            summed = functools.reduce(
                jnp.add,
                [
                    jnp.dot(
                        part.astype(jnp.bfloat16),
                        kv[slot[0], slot[1], 1, :, lanes],
                        preferred_element_type=jnp.float32,
                    )
                    for slot, part in zip(slots, weights)
                ],
            )
            if not first:
                factor = jnp.exp2((old - top) * exponent_scale)
                total = total_ref[h] * factor + total
                summed = summed_ref[h] * factor + summed
            top_ref[h] = top
            total_ref[h] = total
            summed_ref[h] = summed

    def absorb_if(slot, condition):
        guarded(condition, lambda: absorb([slot]))

    def absorb_both(low_slot, high_slot):
        guarded(has_low & has_high, lambda: absorb([low_slot, high_slot]))
        guarded(has_low & jnp.logical_not(has_high), lambda: absorb([low_slot]))
        guarded(has_high & jnp.logical_not(has_low), lambda: absorb([high_slot]))

    absorb([(0, 2)], first=True)
    for half in (0, 1):
        landed((0, 1), half, has_low)
        send("low", half)
        landed((0, 3), half, has_high)
        send("high", half)
        landed((1, 2), half, None)
        send("partner", half)
    absorb_if((1, 2), None)
    for half in (0, 1):
        landed((0, 0), half, has_low2)
        send("low2", half)
        landed((0, 4), half, has_high2)
        send("high2", half)
        if half == 0:
            absorb_both((0, 1), (0, 3))
    absorb_if((0, 0), has_low2)
    absorb_if((0, 4), has_high2)
    for half in (0, 1):
        landed((1, 1), half, has_low)
        landed((1, 3), half, has_high)
    absorb_both((1, 1), (1, 3))
    far_low = has_low2 & (column == 0)
    far_high = has_high2 & (column == 1)
    for slot, condition in (((1, 0), far_low), ((1, 4), far_high)):
        for half in (0, 1):
            landed(slot, half, condition)
        absorb_if(slot, condition)

    for h in range(heads):
        attended_ref[:, h * HEAD_DIM : (h + 1) * HEAD_DIM] = (
            summed_ref[h] / total_ref[h]
        ).astype(jnp.bfloat16)

    opposite = lax.rem(t_me + n_tp // 2, n_tp)
    sibling = t_me + 1 - 2 * lax.rem(t_me, 2)
    diagonal = lax.rem(sibling + n_tp // 2, n_tp)

    def tp_copy(k):
        return pltpu.make_async_remote_copy(
            src_ref=(terms.at[diagonal], terms.at[sibling], pair_sum)[k],
            dst_ref=arrived.at[k],
            send_sem=tp_send.at[k],
            recv_sem=tp_recv.at[k],
            device_id=(me, (sibling, sibling, opposite)[k]),
            device_id_type=MESH,
        )

    loads[4].wait()

    def term(target):
        rows = attended_ref[pl.ds(pl.multiple_of(target * quarter, quarter), quarter), :]
        terms[target] = jnp.dot(
            rows, w_out_ref[...], preferred_element_type=jnp.float32
        ).astype(jnp.bfloat16)

    term(diagonal)
    tp_copy(0).start()
    term(opposite)
    tp_copy(0).wait_recv()
    pair_sum[...] = (
        terms[opposite].astype(jnp.float32) + arrived[0].astype(jnp.float32)
    ).astype(jnp.bfloat16)
    tp_copy(2).start()
    term(sibling)
    tp_copy(1).start()
    term(t_me)

    lanes = max(n_seq, 128)
    own_lane = iota((quarter, quarter), 0) == iota((quarter, quarter), 1)
    owner = jnp.sum(jnp.where(own_lane, owners_ref[...], 0), axis=1, keepdims=True)
    table = (owner == iota((quarter, lanes), 1)).astype(jnp.float32)
    before = (iota((quarter, quarter), 1) < iota((quarter, quarter), 0)).astype(jnp.bfloat16)
    earlier = jnp.dot(before, table.astype(jnp.bfloat16), preferred_element_type=jnp.float32)
    slot = jnp.sum(earlier * table, axis=1, keepdims=True).astype(jnp.int32)
    goal = owner * capacity + slot
    placing = (goal == iota((quarter, n_seq * capacity), 1)).astype(jnp.bfloat16)

    residual = token_rows[
        pl.ds(pl.multiple_of(t_me * quarter, quarter), quarter), :
    ].astype(jnp.float32)
    head_total = terms[t_me].astype(jnp.float32)
    for k in (1, 2):
        tp_copy(k).wait_recv()
        head_total = head_total + arrived[k].astype(jnp.float32)
    residual = residual + head_total + row_of(b_out_ref)
    merged = layer_norm(residual, row_of(merge_gain_ref), row_of(merge_bias_ref)).astype(jnp.bfloat16)
    placed = lax.dot_general(
        placing, merged, (((0,), (0,)), ((), ())), preferred_element_type=jnp.float32
    ).astype(jnp.bfloat16)

    if inside:
        outgoing[...] = placed.reshape(n_seq, capacity, model_width)

        def route(k):
            target = lax.rem(me + k, n_seq)
            return pltpu.make_async_remote_copy(
                src_ref=outgoing.at[target],
                dst_ref=out_ref.at[me],
                send_sem=route_send.at[k],
                recv_sem=route_recv.at[k],
                device_id=(target, t_me),
                device_id_type=MESH,
            )

        def route_in(k):
            source = lax.rem(me + n_seq - k, n_seq)
            return pltpu.make_async_remote_copy(
                src_ref=outgoing.at[source],
                dst_ref=out_ref.at[source],
                send_sem=route_send.at[k],
                recv_sem=route_recv.at[k],
                device_id=(source, t_me),
                device_id_type=MESH,
            )

        order = sorted(range(1, n_seq), key=lambda k: -abs(n_seq // 2 - k))[::-1]
        for k in order:
            route(k).start()
        out_ref[me] = outgoing[me]
    else:
        out_ref[...] = placed

    for name in sends:
        for way, src, dst, *conditions in sends[name]:
            for half in (0, 1):
                guarded(conditions[half], lambda: hop(way, src, dst, half).wait_send())
    for k in range(3):
        tp_copy(k).wait_send()
    if inside:
        for k in order:
            route_in(k).wait_recv()
        for k in order:
            route(k).wait_send()


def per_device(
    tokens, ln_gain, ln_bias, w_qkv, b_qkv, w_out, b_out, merge_gain, merge_bias, segments, owners
):
    tok_dev, model_width = tokens.shape
    local_width = w_qkv.shape[2]
    heads = local_width // HEAD_DIM
    n_seq = lax.axis_size("seq")
    n_tp = lax.axis_size("tp")
    quarter = tok_dev // n_tp
    capacity = max(2, 2 * quarter // n_seq)
    inside = capacity % 16 == 0
    out_shape = (n_seq, capacity, model_width) if inside else (n_seq * capacity, model_width)
    vmem = pl.BlockSpec(memory_space=pltpu.VMEM)
    hbm = pl.BlockSpec(memory_space=pltpu.HBM)
    routed = pl.pallas_call(
        functools.partial(kernel, n_seq, n_tp, capacity, inside),
        out_shape=jax.ShapeDtypeStruct(out_shape, jnp.bfloat16),
        in_specs=[hbm, vmem, vmem, hbm, vmem, hbm] + [vmem] * 5,
        out_specs=vmem,
        scratch_shapes=[
            pltpu.VMEM((tok_dev, model_width), jnp.bfloat16),
            pltpu.VMEM((3, local_width, model_width), jnp.bfloat16),
            pltpu.VMEM((local_width, model_width), jnp.bfloat16),
            pltpu.VMEM((n_seq, 1, tok_dev), jnp.int32),
            pltpu.VMEM((2, 5, 2, tok_dev, local_width), jnp.bfloat16),
            pltpu.VMEM((tok_dev, model_width), jnp.bfloat16),
            pltpu.VMEM((tok_dev, model_width), jnp.bfloat16),
            pltpu.VMEM((tok_dev, local_width), jnp.bfloat16),
            pltpu.VMEM((heads, tok_dev, 1), jnp.float32),
            pltpu.VMEM((heads, tok_dev, 1), jnp.float32),
            pltpu.VMEM((heads, tok_dev, HEAD_DIM), jnp.float32),
            pltpu.VMEM((tok_dev, local_width), jnp.bfloat16),
            pltpu.VMEM((n_tp, quarter, model_width), jnp.bfloat16),
            pltpu.VMEM((3, quarter, model_width), jnp.bfloat16),
            pltpu.VMEM((quarter, model_width), jnp.bfloat16),
            pltpu.VMEM((n_seq, max(capacity, 16), model_width) if inside else (1, 16, 128), jnp.bfloat16),
            pltpu.SemaphoreType.DMA((5,)),
            pltpu.SemaphoreType.DMA((3, 2, 5, 2)),
            pltpu.SemaphoreType.DMA((2, 5, 2)),
            pltpu.SemaphoreType.DMA((3,)),
            pltpu.SemaphoreType.DMA((3,)),
            pltpu.SemaphoreType.DMA((n_seq,)),
            pltpu.SemaphoreType.DMA((n_seq,)),
        ],
        compiler_params=pltpu.CompilerParams(
            collective_id=0, has_side_effects=True, vmem_limit_bytes=60 * 1024 * 1024
        ),
        cost_estimate=pl.CostEstimate(
            flops=2 * 10**9, bytes_accessed=5 * 10**6, transcendentals=3 * 10**6
        ),
    )(
        tokens,
        ln_gain,
        ln_bias,
        jnp.swapaxes(w_qkv, 1, 2),
        b_qkv,
        w_out,
        b_out,
        merge_gain,
        merge_bias,
        segments,
        owners.T,
    )
    if inside:
        return routed.reshape(n_seq * capacity, model_width)
    return lax.all_to_all(routed, "seq", split_axis=0, concat_axis=0, tiled=True)


def solution(mesh):
    placed = (
        P("seq", None),
        P(),
        P(),
        P(None, None, "tp"),
        P(None, "tp"),
        P("tp", None),
        P(),
        P(),
        P(),
        P(),
        P("seq", None),
    )
    return jax.shard_map(
        per_device, mesh=mesh, in_specs=placed, out_specs=P("seq", "tp"), check_vma=False
    )
```

```python
import functools
import math

import jax
import jax.numpy as jnp
from jax import lax
from jax.experimental import pallas as pl
from jax.experimental.pallas import tpu as pltpu
from jax.sharding import PartitionSpec as P

HEAD_DIM = 80
MESH = pl.DeviceIdType.MESH

epsilon = 1e-06
masked_score = -1e30


def layer_norm(values, gain_row, shift_row):
    center = jnp.mean(values, axis=-1, keepdims=True)
    centered = values - center
    spread = jnp.mean(centered * centered, axis=-1, keepdims=True)
    return centered * lax.rsqrt(spread + epsilon) * gain_row + shift_row


def row_of(ref):
    return ref[...].reshape(1, ref.shape[0])


def iota(shape, dim):
    return lax.broadcasted_iota(jnp.int32, shape, dim)


def kernel(
    n_seq,
    n_tp,
    capacity,
    inside,
    tokens_hbm,
    gain_ref,
    bias_ref,
    w_qkv_hbm,
    b_qkv_ref,
    w_out_hbm,
    b_out_ref,
    merge_gain_ref,
    merge_bias_ref,
    segments_ref,
    owners_ref,
    out_ref,
    tokens_ref,
    w_qkv_ref,
    w_out_ref,
    segment_rows,
    kv,
    token_rows,
    normed_ref,
    query_ref,
    top_ref,
    total_ref,
    summed_ref,
    attended_ref,
    terms,
    arrived,
    pair_sum,
    outgoing,
    load_sem,
    kv_send,
    kv_recv,
    tp_send,
    tp_recv,
    route_send,
    route_recv,
):
    tok_dev, model_width = tokens_ref.shape
    local_width = query_ref.shape[1]
    heads = local_width // HEAD_DIM
    quarter = tok_dev // n_tp
    n_pair = n_seq // 2
    me = lax.axis_index("seq")
    t_me = lax.axis_index("tp")
    pair = me // 2
    column = lax.rem(me, 2)
    partner = me + 1 - 2 * column
    has_low = pair > 0
    has_high = pair < n_pair - 1
    has_low2 = pair > 1
    has_high2 = pair < n_pair - 2

    loads = [
        pltpu.make_async_copy(tokens_hbm, tokens_ref, load_sem.at[0]),
        pltpu.make_async_copy(w_qkv_hbm.at[1], w_qkv_ref.at[1], load_sem.at[1]),
        pltpu.make_async_copy(w_qkv_hbm.at[2], w_qkv_ref.at[2], load_sem.at[2]),
        pltpu.make_async_copy(w_qkv_hbm.at[0], w_qkv_ref.at[0], load_sem.at[3]),
        pltpu.make_async_copy(w_out_hbm, w_out_ref, load_sem.at[4]),
    ]
    for load in loads:
        load.start()

    barrier = pltpu.get_barrier_semaphore()
    for k in range(1, n_tp):
        pl.semaphore_signal(
            barrier, inc=1, device_id=(me, lax.rem(t_me + k, n_tp)), device_id_type=MESH
        )
    if inside:
        for k in range(1, n_seq):
            pl.semaphore_signal(
                barrier, inc=1, device_id=(lax.rem(me + k, n_seq), t_me), device_id_type=MESH
            )
    else:
        pl.semaphore_signal(barrier, inc=1, device_id=(partner, t_me), device_id_type=MESH)

        @pl.when(has_low)
        def _():
            pl.semaphore_signal(barrier, inc=1, device_id=(me - 2, t_me), device_id_type=MESH)

        @pl.when(has_high)
        def _():
            pl.semaphore_signal(barrier, inc=1, device_id=(me + 2, t_me), device_id_type=MESH)

    row = iota((tok_dev, tok_dev), 0)
    place = (lax.rem(row, quarter) * n_tp + row // quarter == iota((tok_dev, tok_dev), 1)).astype(
        jnp.bfloat16
    )
    loads[0].wait()
    ordered = jnp.dot(place, tokens_ref[...], preferred_element_type=jnp.float32)
    token_rows[...] = ordered.astype(jnp.bfloat16)
    normed_ref[...] = layer_norm(ordered, row_of(gain_ref), row_of(bias_ref)).astype(jnp.bfloat16)

    def project(i):
        return (
            lax.dot_general(
                normed_ref[...],
                w_qkv_ref[i],
                (((1,), (1,)), ((), ())),
                preferred_element_type=jnp.float32,
            )
            + b_qkv_ref[i : i + 1, :]
        ).astype(jnp.bfloat16)

    loads[1].wait()
    kv[0, 2, 0] = project(1)

    if inside:
        pl.semaphore_wait(barrier, n_tp - 1 + n_seq - 1)
    else:
        pl.semaphore_wait(barrier, n_tp + has_low.astype(jnp.int32) + has_high.astype(jnp.int32))

    def hop(way, src, dst, half):
        target = (me - 2, me + 2, partner)[way]
        return pltpu.make_async_remote_copy(
            src_ref=kv.at[src[0], src[1], half],
            dst_ref=kv.at[dst[0], dst[1], half],
            send_sem=kv_send.at[way, src[0], src[1], half],
            recv_sem=kv_recv.at[dst[0], dst[1], half],
            device_id=(target, t_me),
            device_id_type=MESH,
        )

    low, high, across = 0, 1, 2
    at_first = pair == 0
    at_last = pair == n_pair - 1
    sends = {
        "own": [
            (low, (0, 2), (0, 3), has_low, has_low),
            (high, (0, 2), (0, 1), has_high, has_high),
            (across, (0, 2), (1, 2), None, None),
        ],
        "partner": [
            (high, (1, 2), (1, 1), at_first, at_first | (has_high & (column == 0))),
            (low, (1, 2), (1, 3), at_last, at_last | (has_low & (column == 1))),
        ],
        "low": [
            (high, (0, 1), (0, 0), has_low & has_high, has_low & has_high),
            (
                across,
                (0, 1),
                (1, 1),
                has_low & (pair != 1),
                has_low & (pair != 1) & (column == 0),
            ),
        ],
        "high": [
            (low, (0, 3), (0, 4), has_low & has_high, has_low & has_high),
            (
                across,
                (0, 3),
                (1, 3),
                has_high & (pair != n_pair - 2),
                has_high & (pair != n_pair - 2) & (column == 1),
            ),
        ],
        "low2": [
            (across, (0, 0), (1, 0), has_low2 & (column == 1), has_low2 & (column == 1))
        ],
        "high2": [
            (across, (0, 4), (1, 4), has_high2 & (column == 0), has_high2 & (column == 0))
        ],
    }

    def guarded(condition, action):
        if condition is None:
            action()
        else:
            pl.when(condition)(action)

    def send(name, half):
        for way, src, dst, *conditions in sends[name]:
            guarded(conditions[half], lambda: hop(way, src, dst, half).start())

    def landed(slot, half, condition):
        guarded(condition, lambda: hop(across, slot, slot, half).wait_recv())

    send("own", 0)
    loads[2].wait()
    kv[0, 2, 1] = project(2)
    send("own", 1)
    loads[3].wait()
    query_ref[...] = project(0)

    segments = row_of(segments_ref)
    for block in range(n_seq):
        segment_rows[block] = jnp.concatenate(
            [segments[:, block * quarter : (block + 1) * quarter]] * n_tp, axis=1
        )

    def segment_row(block):
        return segment_rows[block]

    exponent_scale = HEAD_DIM ** (-0.5) * math.log2(math.e)
    own_row = segment_row(me)
    eye = row == iota((tok_dev, tok_dev), 1)
    own_segment = jnp.sum(jnp.where(eye, own_row, 0), axis=1, keepdims=True)

    def block_of(slot):
        return 2 * (pair + slot[1] - 2) + (column if slot[0] == 0 else 1 - column)

    def absorb(slots, first=False):
        allowed = [
            jnp.where(own_segment == segment_row(block_of(slot)), 0.0, masked_score)
            for slot in slots
        ]
        for h in range(heads):
            lanes = slice(h * HEAD_DIM, (h + 1) * HEAD_DIM)
            query = query_ref[:, lanes]
            scores = [
                lax.dot_general(
                    query,
                    kv[slot[0], slot[1], 0, :, lanes],
                    (((1,), (1,)), ((), ())),
                    preferred_element_type=jnp.float32,
                )
                + mask
                for slot, mask in zip(slots, allowed)
            ]
            top = jnp.max(functools.reduce(jnp.maximum, scores), axis=1, keepdims=True)
            if not first:
                old = top_ref[h]
                top = jnp.maximum(old, top)
            weights = [jnp.exp2((part - top) * exponent_scale) for part in scores]
            total = jnp.sum(functools.reduce(jnp.add, weights), axis=1, keepdims=True)
            summed = functools.reduce(
                jnp.add,
                [
                    jnp.dot(
                        part.astype(jnp.bfloat16),
                        kv[slot[0], slot[1], 1, :, lanes],
                        preferred_element_type=jnp.float32,
                    )
                    for slot, part in zip(slots, weights)
                ],
            )
            if not first:
                factor = jnp.exp2((old - top) * exponent_scale)
                total = total_ref[h] * factor + total
                summed = summed_ref[h] * factor + summed
            top_ref[h] = top
            total_ref[h] = total
            summed_ref[h] = summed

    def absorb_if(slot, condition):
        guarded(condition, lambda: absorb([slot]))

    def absorb_both(low_slot, high_slot):
        guarded(has_low & has_high, lambda: absorb([low_slot, high_slot]))
        guarded(has_low & jnp.logical_not(has_high), lambda: absorb([low_slot]))
        guarded(has_high & jnp.logical_not(has_low), lambda: absorb([high_slot]))

    absorb([(0, 2)], first=True)
    for half in (0, 1):
        landed((0, 1), half, has_low)
        send("low", half)
        landed((0, 3), half, has_high)
        send("high", half)
        landed((1, 2), half, None)
        send("partner", half)
    absorb_if((1, 2), None)
    for half in (0, 1):
        landed((0, 0), half, has_low2)
        send("low2", half)
        landed((0, 4), half, has_high2)
        send("high2", half)
        if half == 0:
            absorb_both((0, 1), (0, 3))
    absorb_if((0, 0), has_low2)
    absorb_if((0, 4), has_high2)
    for half in (0, 1):
        landed((1, 1), half, has_low)
        landed((1, 3), half, has_high)
    absorb_both((1, 1), (1, 3))
    far_low = has_low2 & (column == 0)
    far_high = has_high2 & (column == 1)
    for slot, condition in (((1, 0), far_low), ((1, 4), far_high)):
        for half in (0, 1):
            landed(slot, half, condition)
        absorb_if(slot, condition)

    for h in range(heads):
        attended_ref[:, h * HEAD_DIM : (h + 1) * HEAD_DIM] = (
            summed_ref[h] / total_ref[h]
        ).astype(jnp.bfloat16)

    opposite = lax.rem(t_me + n_tp // 2, n_tp)
    sibling = t_me + 1 - 2 * lax.rem(t_me, 2)
    diagonal = lax.rem(sibling + n_tp // 2, n_tp)

    def tp_copy(k):
        return pltpu.make_async_remote_copy(
            src_ref=(terms.at[diagonal], terms.at[sibling], pair_sum)[k],
            dst_ref=arrived.at[k],
            send_sem=tp_send.at[k],
            recv_sem=tp_recv.at[k],
            device_id=(me, (sibling, sibling, opposite)[k]),
            device_id_type=MESH,
        )

    loads[4].wait()

    def term(target):
        rows = attended_ref[pl.ds(pl.multiple_of(target * quarter, quarter), quarter), :]
        terms[target] = jnp.dot(
            rows, w_out_ref[...], preferred_element_type=jnp.float32
        ).astype(jnp.bfloat16)

    term(diagonal)
    tp_copy(0).start()
    term(opposite)
    tp_copy(0).wait_recv()
    pair_sum[...] = (
        terms[opposite].astype(jnp.float32) + arrived[0].astype(jnp.float32)
    ).astype(jnp.bfloat16)
    tp_copy(2).start()
    term(sibling)
    tp_copy(1).start()
    term(t_me)

    lanes = max(n_seq, 128)
    own_lane = iota((quarter, quarter), 0) == iota((quarter, quarter), 1)
    owner = jnp.sum(jnp.where(own_lane, owners_ref[...], 0), axis=1, keepdims=True)
    table = (owner == iota((quarter, lanes), 1)).astype(jnp.float32)
    before = (iota((quarter, quarter), 1) < iota((quarter, quarter), 0)).astype(jnp.bfloat16)
    earlier = jnp.dot(before, table.astype(jnp.bfloat16), preferred_element_type=jnp.float32)
    slot = jnp.sum(earlier * table, axis=1, keepdims=True).astype(jnp.int32)
    goal = owner * capacity + slot
    placing = (goal == iota((quarter, n_seq * capacity), 1)).astype(jnp.bfloat16)

    residual = token_rows[
        pl.ds(pl.multiple_of(t_me * quarter, quarter), quarter), :
    ].astype(jnp.float32)
    head_total = terms[t_me].astype(jnp.float32)
    for k in (1, 2):
        tp_copy(k).wait_recv()
        head_total = head_total + arrived[k].astype(jnp.float32)
    residual = residual + head_total + row_of(b_out_ref)
    merged = layer_norm(residual, row_of(merge_gain_ref), row_of(merge_bias_ref)).astype(jnp.bfloat16)
    placed = lax.dot_general(
        placing, merged, (((0,), (0,)), ((), ())), preferred_element_type=jnp.float32
    ).astype(jnp.bfloat16)

    if inside:
        outgoing[...] = placed.reshape(n_seq, capacity, model_width)

        def route(k):
            target = lax.rem(me + k, n_seq)
            return pltpu.make_async_remote_copy(
                src_ref=outgoing.at[target],
                dst_ref=out_ref.at[me],
                send_sem=route_send.at[k],
                recv_sem=route_recv.at[k],
                device_id=(target, t_me),
                device_id_type=MESH,
            )

        def route_in(k):
            source = lax.rem(me + n_seq - k, n_seq)
            return pltpu.make_async_remote_copy(
                src_ref=outgoing.at[source],
                dst_ref=out_ref.at[source],
                send_sem=route_send.at[k],
                recv_sem=route_recv.at[k],
                device_id=(source, t_me),
                device_id_type=MESH,
            )

        order = sorted(range(1, n_seq), key=lambda k: -abs(n_seq // 2 - k))[::-1]
        for k in order:
            route(k).start()
        out_ref[me] = outgoing[me]
    else:
        out_ref[...] = placed

    for name in sends:
        for way, src, dst, *conditions in sends[name]:
            for half in (0, 1):
                guarded(conditions[half], lambda: hop(way, src, dst, half).wait_send())
    for k in range(3):
        tp_copy(k).wait_send()
    if inside:
        for k in order:
            route_in(k).wait_recv()
        for k in order:
            route(k).wait_send()


def per_device(
    tokens, ln_gain, ln_bias, w_qkv, b_qkv, w_out, b_out, merge_gain, merge_bias, segments, owners
):
    tok_dev, model_width = tokens.shape
    local_width = w_qkv.shape[2]
    heads = local_width // HEAD_DIM
    n_seq = lax.axis_size("seq")
    n_tp = lax.axis_size("tp")
    quarter = tok_dev // n_tp
    capacity = max(2, 2 * quarter // n_seq)
    inside = capacity % 16 == 0
    out_shape = (n_seq, capacity, model_width) if inside else (n_seq * capacity, model_width)
    vmem = pl.BlockSpec(memory_space=pltpu.VMEM)
    hbm = pl.BlockSpec(memory_space=pltpu.HBM)
    routed = pl.pallas_call(
        functools.partial(kernel, n_seq, n_tp, capacity, inside),
        out_shape=jax.ShapeDtypeStruct(out_shape, jnp.bfloat16),
        in_specs=[hbm, vmem, vmem, hbm, vmem, hbm] + [vmem] * 5,
        out_specs=vmem,
        scratch_shapes=[
            pltpu.VMEM((tok_dev, model_width), jnp.bfloat16),
            pltpu.VMEM((3, local_width, model_width), jnp.bfloat16),
            pltpu.VMEM((local_width, model_width), jnp.bfloat16),
            pltpu.VMEM((n_seq, 1, tok_dev), jnp.int32),
            pltpu.VMEM((2, 5, 2, tok_dev, local_width), jnp.bfloat16),
            pltpu.VMEM((tok_dev, model_width), jnp.bfloat16),
            pltpu.VMEM((tok_dev, model_width), jnp.bfloat16),
            pltpu.VMEM((tok_dev, local_width), jnp.bfloat16),
            pltpu.VMEM((heads, tok_dev, 1), jnp.float32),
            pltpu.VMEM((heads, tok_dev, 1), jnp.float32),
            pltpu.VMEM((heads, tok_dev, HEAD_DIM), jnp.float32),
            pltpu.VMEM((tok_dev, local_width), jnp.bfloat16),
            pltpu.VMEM((n_tp, quarter, model_width), jnp.bfloat16),
            pltpu.VMEM((3, quarter, model_width), jnp.bfloat16),
            pltpu.VMEM((quarter, model_width), jnp.bfloat16),
            pltpu.VMEM((n_seq, max(capacity, 16), model_width) if inside else (1, 16, 128), jnp.bfloat16),
            pltpu.SemaphoreType.DMA((5,)),
            pltpu.SemaphoreType.DMA((3, 2, 5, 2)),
            pltpu.SemaphoreType.DMA((2, 5, 2)),
            pltpu.SemaphoreType.DMA((3,)),
            pltpu.SemaphoreType.DMA((3,)),
            pltpu.SemaphoreType.DMA((n_seq,)),
            pltpu.SemaphoreType.DMA((n_seq,)),
        ],
        compiler_params=pltpu.CompilerParams(
            collective_id=0, has_side_effects=True, vmem_limit_bytes=60 * 1024 * 1024
        ),
        cost_estimate=pl.CostEstimate(
            flops=2 * 10**9, bytes_accessed=5 * 10**6, transcendentals=3 * 10**6
        ),
    )(
        tokens,
        ln_gain,
        ln_bias,
        jnp.swapaxes(w_qkv, 1, 2),
        b_qkv,
        w_out,
        b_out,
        merge_gain,
        merge_bias,
        segments,
        owners.T,
    )
    if inside:
        return routed.reshape(n_seq * capacity, model_width)
    return lax.all_to_all(routed, "seq", split_axis=0, concat_axis=0, tiled=True)


def solution(mesh):
    placed = (
        P("seq", None),
        P(),
        P(),
        P(None, None, "tp"),
        P(None, "tp"),
        P("tp", None),
        P(),
        P(),
        P(),
        P(),
        P("seq", None),
    )
    return jax.shard_map(
        per_device, mesh=mesh, in_specs=placed, out_specs=P("seq", "tp"), check_vma=False
    )
```
